32 devices in a mesh: dp: 4 (over y, x), mp: 8 (over z, core).
Axes of the slice: x: 2, y: 2, z: 4, core: 2. Of those that a mesh axis runs over, the one named last changes fastest.
Arguments:
- hidden: bfloat16 [512, 28672], P(None, 'mp'), may hold values from -0.25 to 0.25
- grad_out: bfloat16 [512, 16384], P('mp', 'dp'), may hold values from -6 to 6
- down_weight: bfloat16 [28672, 16384], P('mp', 'dp'), may hold values from -0.03125 to 0.03125
Outputs:
- grad_hidden: bfloat16 [512, 28672], P('dp', 'mp')
- grad_weight: bfloat16 [28672, 16384], P('mp', 'dp')
The draws below stay inside these ranges and needn't reach their ends.
All inputs are finite; a program needn't handle non-finite values.
Results may differ from the reference program's by a relative error of at most 0.012.
Values may be sent and summed in bfloat16 or wider, within the bound.
A program may use at most 128 MiB of HBM per device.

```python
import jax
import jax.numpy as jnp
from jax import lax

D = 16384
FF = 28672
TOKENS = 512
N_DP = 4


def strengthened(array, stream_key, source, target, shards_of, factor):
    def block_of(position):
        return (jnp.arange(array.shape[position]) // (array.shape[position] // shards_of)).reshape((-1,) + (1,) * (array.ndim - 1 - position))

    one_side = jax.random.permutation(stream_key, shards_of)[block_of(target)]
    other_side = (block_of(target) + shards_of // 2) % shards_of
    return jnp.where((block_of(source) == one_side) | (block_of(source) == other_side), factor * array, array)


def steps_of(key, shape, split, least, high):
    factor_of, own = 1.0, jax.random.fold_in(key, 6)
    for position, shards_of in split:
        heights = jnp.exp(jax.random.uniform(jax.random.fold_in(own, position), (shards_of,), jnp.float32, least / len(split), high / len(split)))
        factor_of = factor_of * jnp.repeat(heights, shape[position] // shards_of).reshape([-1 if axis == position else 1 for axis in range(len(shape))])
    return factor_of


def centred(key, dims, width, limit, shards=(), held_as=jnp.bfloat16):
    drawn = jax.random.normal(key, dims, jnp.float32) * width
    if len(shards) > 0:
        drawn = steps_of(key, dims, shards, -0.22, 0.18) * drawn
    return jnp.clip(drawn, min=-limit, max=limit).astype(held_as)


def gaussian_with(stream_key, dims, deviation, limit, shards, heavy, held_as=jnp.bfloat16):
    drawn = deviation * jax.random.normal(stream_key, dims, jnp.float32)
    if shards:
        drawn = drawn * steps_of(stream_key, dims, shards, -0.22, 0.18)
    return jnp.clip(strengthened(drawn, jax.random.fold_in(stream_key, 3), *heavy), -limit, limit).astype(held_as)


def setup_inputs(seed: int = 0) -> dict:
    splits = jax.random.split(jax.random.key(seed), 4)
    return {
        "hidden": centred(splits[0], (TOKENS, FF), TOKENS ** -0.5, 0.25, ((1, 8),)),
        "grad_out": gaussian_with(splits[1], (TOKENS, D), 1.0, 6.0, ((0, 8), (1, 4)), (1, 0, 8, 2.0)),
        "down_weight": centred(splits[2], (FF, D), FF ** -0.5, 0.03125, ((0, 8), (1, 4))),
    }


def reference(hidden, grad_out, down_weight):
    slab_width = D // N_DP
    summed = jnp.zeros((TOKENS, FF), jnp.float32)
    for block_index in range(N_DP):
        grad_slab = grad_out[:, block_index * slab_width:(block_index + 1) * slab_width]
        weight_slab = down_weight[:, block_index * slab_width:(block_index + 1) * slab_width]
        partial_value = lax.dot_general(grad_slab, weight_slab, (((1,), (1,)), ((), ())), preferred_element_type=jnp.float32).astype(jnp.bfloat16)
        partial_value = lax.optimization_barrier(partial_value)
        summed = summed + partial_value.astype(jnp.float32)
    grad_weight = lax.dot_general(hidden, grad_out, (((0,), (0,)), ((), ())), preferred_element_type=jnp.float32)
    return summed.astype(jnp.bfloat16), grad_weight.astype(jnp.bfloat16)
```

```python
import functools

import jax
import jax.numpy as jnp
from jax import lax
from jax.experimental import pallas as pl
from jax.experimental.pallas import tpu as pltpu
from jax.sharding import PartitionSpec as P

ROWS = 16
MESH = pl.DeviceIdType.MESH


def gather_kernel(n_dp, n_mp, rounds, kernel_rounds, chunk,
                  g_ref, w_ref, panel_out, part_out, gh_out,
                  panel, w, part, arrived,
                  g_sem, w_sem, panel_sem, part_sem,
                  z_send, z_recv, sib_send, sib_recv, rs_send, rs_recv):
    d = lax.axis_index("dp")
    me = lax.axis_index("mp")
    chip = me // 2
    core = lax.rem(me, 2)
    sibling = me + 1 - 2 * core
    chips = n_mp // 2
    per_owner = n_mp // n_dp
    chunks = w.shape[0] // chunk

    g_copy = pltpu.make_async_copy(g_ref, panel.at[:, me], g_sem)
    g_copy.start()

    def w_copy(i):
        rows = pl.ds(pl.multiple_of(i * chunk, chunk), chunk)
        return pltpu.make_async_copy(w_ref.at[rows, :], w.at[rows, :], w_sem.at[i])

    @pl.loop(0, chunks)
    def _(i):
        w_copy(i).start()

    barrier = pltpu.get_barrier_semaphore()

    def greet(dp, mp):
        pl.semaphore_signal(barrier, inc=1, device_id=(dp, mp), device_id_type=MESH)

    greet(d, sibling)

    @pl.when(chip > 0)
    def _():
        greet(d, me - 2)

    @pl.when(chip < chips - 1)
    def _():
        greet(d, me + 2)

    for j in range(n_dp - 1):
        greet(lax.rem(d + j + 1, n_dp), me)
    heard = n_dp + jnp.where(chip > 0, 1, 0) + jnp.where(chip < chips - 1, 1, 0)
    pl.semaphore_wait(barrier, heard)
    g_copy.wait()

    def z_copy(r, way, k, m):
        return pltpu.make_async_remote_copy(
            src_ref=panel.at[r, m], dst_ref=panel.at[r, m],
            send_sem=z_send.at[r, way, k], recv_sem=z_recv.at[r, way, k],
            device_id=(d, me - 2 if way == 0 else me + 2), device_id_type=MESH)

    def sib_copy(r, way, k, m):
        return pltpu.make_async_remote_copy(
            src_ref=panel.at[r, m], dst_ref=panel.at[r, m],
            send_sem=sib_send.at[r, way, k], recv_sem=sib_recv.at[r, way, k],
            device_id=(d, sibling), device_id_type=MESH)

    def further(way):
        return chip > 0 if way == 0 else chip < chips - 1

    def inside(way, k):
        return chip + k < chips if way == 0 else chip - k >= 0

    def source(way, k):
        return chip + k if way == 0 else chip - k

    def send_own(r):
        for way in range(2):
            @pl.when(further(way))
            def _():
                z_copy(r, way, 1, me).start()
        sib_copy(r, 0, 0, me).start()

    def forward(r, k):
        for way in range(2):
            @pl.when(inside(way, k))
            def _():
                m = 2 * source(way, k) + core
                z_copy(r, way, k, m).wait_recv()

                @pl.when(further(way))
                def _():
                    z_copy(r, way, k + 1, m).start()

                sib_copy(r, way, k, m).start()

    def wait_siblings(r):
        sib_copy(r, 0, 0, sibling).wait_recv()

        @pl.loop(1, chips)
        def _(k):
            for way in range(2):
                @pl.when(inside(way, k))
                def _():
                    sib_copy(r, way, k, 2 * source(way, k) + 1 - core).wait_recv()

    def panel_copy(r):
        return pltpu.make_async_copy(panel.at[r], panel_out.at[:, r], panel_sem.at[r])

    def part_copy(r):
        return pltpu.make_async_copy(
            part.at[r], part_out.at[:, r - kernel_rounds], part_sem.at[r])

    def rs_copy(r, j):
        owner = lax.rem(d + j + 1, n_dp)
        return pltpu.make_async_remote_copy(
            src_ref=part.at[r, pl.ds(owner * per_owner, per_owner)],
            dst_ref=arrived.at[j, r],
            send_sem=rs_send.at[j, r], recv_sem=rs_recv.at[j, r],
            device_id=(owner, me), device_id_type=MESH)

    send_own(0)
    if rounds > 1:
        send_own(1)

    @pl.loop(1, chips)
    def _(k):
        forward(0, k)

    def send_part(r):
        @pl.when(r < kernel_rounds)
        def _():
            for j in range(n_dp - 1):
                rs_copy(r, j).start()

        @pl.when(r >= kernel_rounds)
        def _():
            part_copy(r).start()

    groups = chips - 1

    @pl.loop(0, rounds)
    def _(r):
        @pl.when(r + 2 < rounds)
        def _():
            send_own(r + 2)

        wait_siblings(r)
        panel_copy(r).start()

        @pl.loop(0, groups)
        def _(k):
            @pl.loop(chunks * k // groups, chunks * (k + 1) // groups)
            def _(i):
                @pl.when(r == 0)
                def _():
                    w_copy(i).wait()

                cols = pl.ds(pl.multiple_of(i * chunk, chunk), chunk)
                a = panel[r].reshape(n_mp * ROWS, panel.shape[-1])
                out = lax.dot_general(a, w[cols, :], (((1,), (1,)), ((), ())),
                                      preferred_element_type=jnp.float32)
                part[r, :, :, cols] = out.astype(part.dtype).reshape(n_mp, ROWS, chunk)

            @pl.when(k == groups - 1)
            def _():
                send_part(r)

            @pl.when(r + 1 < rounds)
            def _():
                forward(r + 1, k + 1)

    for r in range(kernel_rounds):
        for j in range(n_dp - 1):
            rs_copy(r, j).wait_recv()

        @pl.loop(0, chunks)
        def _(i):
            cols = pl.ds(pl.multiple_of(i * chunk, chunk), chunk)
            total = part[r, pl.ds(d * per_owner, per_owner), :, cols].astype(jnp.float32)
            for j in range(n_dp - 1):
                total += arrived[j, r, :, :, cols].astype(jnp.float32)
            gh_out[:, r, :, cols] = total.astype(gh_out.dtype)

    @pl.loop(0, rounds)
    def _(r):
        panel_copy(r).wait()
        sib_copy(r, 0, 0, me).wait_send()
        for way in range(2):
            @pl.when(further(way))
            def _():
                z_copy(r, way, 1, me).wait_send()

        @pl.loop(1, chips)
        def _(k):
            for way in range(2):
                @pl.when(inside(way, k))
                def _():
                    m = 2 * source(way, k) + core
                    sib_copy(r, way, k, m).wait_send()

                    @pl.when(further(way))
                    def _():
                        z_copy(r, way, k + 1, m).wait_send()

        @pl.when(r < kernel_rounds)
        def _():
            for j in range(n_dp - 1):
                rs_copy(r, j).wait_send()

        @pl.when(r >= kernel_rounds)
        def _():
            part_copy(r).wait()


def weight_kernel(tile, h_ref, g_ref, out_ref):
    h = h_ref[...]

    @pl.loop(0, out_ref.shape[1] // tile)
    def _(i):
        cols = pl.ds(pl.multiple_of(i * tile, tile), tile)
        out_ref[:, cols] = lax.dot_general(
            h, g_ref[:, cols], (((0,), (0,)), ((), ())),
            preferred_element_type=jnp.float32).astype(out_ref.dtype)


def weight_gradient(hidden, panel):
    tokens, units = hidden.shape
    width = panel.shape[1]
    block = next(c for c in (256, 128) if units % c == 0)
    return pl.pallas_call(
        functools.partial(weight_kernel, min(width, 1024)),
        grid=(units // block,),
        out_shape=jax.ShapeDtypeStruct((units, width), hidden.dtype),
        in_specs=[
            pl.BlockSpec((tokens, block), lambda i: (0, i)),
            pl.BlockSpec((tokens, width), lambda i: (0, 0)),
        ],
        out_specs=pl.BlockSpec((block, width), lambda i: (i, 0)),
        compiler_params=pltpu.CompilerParams(vmem_limit_bytes=48 * 1024 * 1024),
        cost_estimate=pl.CostEstimate(
            flops=2 * tokens * width * units, transcendentals=0,
            bytes_accessed=2 * units * width),
    )(hidden, panel)


def per_device(n_dp, n_mp, hidden, grad_out, down_weight):
    rows, width = grad_out.shape
    units = down_weight.shape[0]
    tokens = rows * n_mp
    rounds = rows // ROWS
    kernel_rounds = rounds - rounds // 4
    rest = rounds - kernel_rounds
    chips = n_mp // 2
    per_owner = n_mp // n_dp
    chunk = next(c for c in (512, 256, 128) if units % c == 0)
    chunks = units // chunk
    bf16 = jnp.bfloat16
    dma = pltpu.SemaphoreType.DMA

    panel, part, gh = pl.pallas_call(
        functools.partial(gather_kernel, n_dp, n_mp, rounds, kernel_rounds, chunk),
        out_shape=(
            jax.ShapeDtypeStruct((n_mp, rounds, ROWS, width), bf16),
            jax.ShapeDtypeStruct((n_mp, rest, ROWS, units), bf16),
            jax.ShapeDtypeStruct((per_owner, kernel_rounds, ROWS, units), bf16),
        ),
        in_specs=[pl.BlockSpec(memory_space=pl.ANY)] * 2,
        out_specs=(
            pl.BlockSpec(memory_space=pl.ANY),
            pl.BlockSpec(memory_space=pl.ANY),
            pl.BlockSpec(memory_space=pltpu.VMEM),
        ),
        scratch_shapes=[
            pltpu.VMEM((rounds, n_mp, ROWS, width), bf16),
            pltpu.VMEM((units, width), bf16),
            pltpu.VMEM((rounds, n_mp, ROWS, units), bf16),
            pltpu.VMEM((n_dp - 1, kernel_rounds, per_owner, ROWS, units), bf16),
            dma, dma((chunks,)), dma((rounds,)), dma((rounds,)),
            dma((rounds, 2, chips)), dma((rounds, 2, chips)),
            dma((rounds, 2, chips)), dma((rounds, 2, chips)),
            dma((n_dp - 1, kernel_rounds)), dma((n_dp - 1, kernel_rounds)),
        ],
        compiler_params=pltpu.CompilerParams(
            collective_id=0, has_side_effects=True, vmem_limit_bytes=56 * 1024 * 1024),
        cost_estimate=pl.CostEstimate(
            flops=2 * tokens * width * units, transcendentals=0,
            bytes_accessed=2 * units * width),
    )(grad_out.reshape(rounds, ROWS, width), down_weight)

    scattered = lax.psum_scatter(
        part.reshape(n_mp * rest * ROWS, units), "dp", scatter_dimension=0, tiled=True)
    grad_weight = weight_gradient(hidden, panel.reshape(tokens, width))
    grad_hidden = jnp.concatenate(
        [gh.reshape(per_owner, kernel_rounds * ROWS, units),
         scattered.reshape(per_owner, rest * ROWS, units)], axis=1)
    return grad_hidden.reshape(tokens // n_dp, units), grad_weight


def solution(mesh):
    return jax.shard_map(
        functools.partial(per_device, mesh.shape["dp"], mesh.shape["mp"]),
        mesh=mesh,
        in_specs=(P(None, "mp"), P("mp", "dp"), P("mp", "dp")),
        out_specs=(P("dp", "mp"), P("mp", "dp")),
        check_vma=False,
    )
```

```python
import functools

import jax
import jax.numpy as jnp
from jax import lax
from jax.experimental import pallas as pl
from jax.experimental.pallas import tpu as pltpu
from jax.sharding import PartitionSpec as P

ROWS = 32
MESH = pl.DeviceIdType.MESH


def gather_kernel(n_dp, n_mp, rounds, chunk,
                  g_ref, w_ref, panel_out, gh_out,
                  panel, w, part, arrived,
                  g_sem, w_sem, panel_sem,
                  z_send, z_recv, sib_send, sib_recv, rs_send, rs_recv):
    d = lax.axis_index("dp")
    me = lax.axis_index("mp")
    chip = me // 2
    core = lax.rem(me, 2)
    sibling = me + 1 - 2 * core
    chips = n_mp // 2
    per_owner = n_mp // n_dp
    chunks = w.shape[0] // chunk

    g_copy = pltpu.make_async_copy(g_ref, panel.at[:, me], g_sem)
    g_copy.start()

    def w_copy(i):
        rows = pl.ds(pl.multiple_of(i * chunk, chunk), chunk)
        return pltpu.make_async_copy(w_ref.at[rows, :], w.at[rows, :], w_sem.at[i])

    @pl.loop(0, chunks)
    def _(i):
        w_copy(i).start()

    barrier = pltpu.get_barrier_semaphore()

    def greet(dp, mp):
        pl.semaphore_signal(barrier, inc=1, device_id=(dp, mp), device_id_type=MESH)

    greet(d, sibling)

    @pl.when(chip > 0)
    def _():
        greet(d, me - 2)

    @pl.when(chip < chips - 1)
    def _():
        greet(d, me + 2)

    for j in range(n_dp - 1):
        greet(lax.rem(d + j + 1, n_dp), me)
    heard = n_dp + jnp.where(chip > 0, 1, 0) + jnp.where(chip < chips - 1, 1, 0)
    pl.semaphore_wait(barrier, heard)
    g_copy.wait()

    def z_copy(r, way, k, m):
        return pltpu.make_async_remote_copy(
            src_ref=panel.at[r, m], dst_ref=panel.at[r, m],
            send_sem=z_send.at[r, way, k], recv_sem=z_recv.at[r, way, k],
            device_id=(d, me - 2 if way == 0 else me + 2), device_id_type=MESH)

    def sib_copy(r, way, k, m):
        return pltpu.make_async_remote_copy(
            src_ref=panel.at[r, m], dst_ref=panel.at[r, m],
            send_sem=sib_send.at[r, way, k], recv_sem=sib_recv.at[r, way, k],
            device_id=(d, sibling), device_id_type=MESH)

    def further(way):
        return chip > 0 if way == 0 else chip < chips - 1

    def inside(way, k):
        return chip + k < chips if way == 0 else chip - k >= 0

    def source(way, k):
        return chip + k if way == 0 else chip - k

    def send_own(r):
        for way in range(2):
            @pl.when(further(way))
            def _():
                z_copy(r, way, 1, me).start()
        sib_copy(r, 0, 0, me).start()

    def forward(r, k):
        for way in range(2):
            @pl.when(inside(way, k))
            def _():
                m = 2 * source(way, k) + core
                z_copy(r, way, k, m).wait_recv()

                @pl.when(further(way))
                def _():
                    z_copy(r, way, k + 1, m).start()

                sib_copy(r, way, k, m).start()

    def wait_siblings(r):
        sib_copy(r, 0, 0, sibling).wait_recv()

        @pl.loop(1, chips)
        def _(k):
            for way in range(2):
                @pl.when(inside(way, k))
                def _():
                    sib_copy(r, way, k, 2 * source(way, k) + 1 - core).wait_recv()

    def panel_copy(r):
        return pltpu.make_async_copy(panel.at[r], panel_out.at[:, r], panel_sem.at[r])

    def rs_copy(r, j, i):
        cols = pl.ds(pl.multiple_of(i * chunk, chunk), chunk)
        owner = lax.rem(d + j + 1, n_dp)
        return pltpu.make_async_remote_copy(
            src_ref=part.at[r, pl.ds(owner * per_owner, per_owner), :, cols],
            dst_ref=arrived.at[j, r, :, :, cols],
            send_sem=rs_send.at[j, r, i], recv_sem=rs_recv.at[j, r, i],
            device_id=(owner, me), device_id_type=MESH)

    send_own(0)
    if rounds > 1:
        send_own(1)

    @pl.loop(1, chips)
    def _(k):
        forward(0, k)

    groups = chips - 1

    @pl.loop(0, rounds)
    def _(r):
        @pl.when(r + 2 < rounds)
        def _():
            send_own(r + 2)

        wait_siblings(r)
        panel_copy(r).start()

        @pl.loop(0, groups)
        def _(k):
            @pl.loop(chunks * k // groups, chunks * (k + 1) // groups)
            def _(i):
                @pl.when(r == 0)
                def _():
                    w_copy(i).wait()

                cols = pl.ds(pl.multiple_of(i * chunk, chunk), chunk)
                a = panel[r].reshape(n_mp * ROWS, panel.shape[-1])
                out = lax.dot_general(a, w[cols, :], (((1,), (1,)), ((), ())),
                                      preferred_element_type=jnp.float32)
                part[r, :, :, cols] = out.astype(part.dtype).reshape(n_mp, ROWS, chunk)
                for j in range(n_dp - 1):
                    rs_copy(r, j, i).start()

            @pl.when(r + 1 < rounds)
            def _():
                forward(r + 1, k + 1)

    for r in range(rounds):
        @pl.loop(0, chunks)
        def _(i):
            for j in range(n_dp - 1):
                rs_copy(r, j, i).wait_recv()
            cols = pl.ds(pl.multiple_of(i * chunk, chunk), chunk)
            total = part[r, pl.ds(d * per_owner, per_owner), :, cols].astype(jnp.float32)
            for j in range(n_dp - 1):
                total += arrived[j, r, :, :, cols].astype(jnp.float32)
            gh_out[:, r, :, cols] = total.astype(gh_out.dtype)

    @pl.loop(0, rounds)
    def _(r):
        panel_copy(r).wait()
        sib_copy(r, 0, 0, me).wait_send()
        for way in range(2):
            @pl.when(further(way))
            def _():
                z_copy(r, way, 1, me).wait_send()

        @pl.loop(1, chips)
        def _(k):
            for way in range(2):
                @pl.when(inside(way, k))
                def _():
                    m = 2 * source(way, k) + core
                    sib_copy(r, way, k, m).wait_send()

                    @pl.when(further(way))
                    def _():
                        z_copy(r, way, k + 1, m).wait_send()

        @pl.loop(0, chunks)
        def _(i):
            for j in range(n_dp - 1):
                rs_copy(r, j, i).wait_send()


def weight_kernel(tile, h_ref, g_ref, out_ref, h):
    h[...] = h_ref[...].T

    @pl.loop(0, out_ref.shape[1] // tile)
    def _(i):
        cols = pl.ds(pl.multiple_of(i * tile, tile), tile)
        out_ref[:, cols] = lax.dot_general(
            h[...], g_ref[:, cols], (((1,), (0,)), ((), ())),
            preferred_element_type=jnp.float32).astype(out_ref.dtype)


def weight_gradient(hidden, panel):
    tokens, units = hidden.shape
    width = panel.shape[1]
    block = next(c for c in (512, 256, 128) if units % c == 0)
    return pl.pallas_call(
        functools.partial(weight_kernel, min(width, 512)),
        grid=(units // block,),
        out_shape=jax.ShapeDtypeStruct((units, width), hidden.dtype),
        in_specs=[
            pl.BlockSpec((tokens, block), lambda i: (0, i)),
            pl.BlockSpec((tokens, width), lambda i: (0, 0)),
        ],
        out_specs=pl.BlockSpec((block, width), lambda i: (i, 0)),
        scratch_shapes=[pltpu.VMEM((block, tokens), hidden.dtype)],
        compiler_params=pltpu.CompilerParams(vmem_limit_bytes=61 * 1024 * 1024),
        cost_estimate=pl.CostEstimate(
            flops=2 * tokens * width * units, transcendentals=0,
            bytes_accessed=2 * units * width),
    )(hidden, panel)


def per_device(n_dp, n_mp, hidden, grad_out, down_weight):
    rows, width = grad_out.shape
    units = down_weight.shape[0]
    tokens = rows * n_mp
    rounds = rows // ROWS
    chips = n_mp // 2
    per_owner = n_mp // n_dp
    chunk = next(c for c in (512, 256, 128) if units % c == 0)
    chunks = units // chunk
    bf16 = jnp.bfloat16
    dma = pltpu.SemaphoreType.DMA

    panel, gh = pl.pallas_call(
        functools.partial(gather_kernel, n_dp, n_mp, rounds, chunk),
        out_shape=(
            jax.ShapeDtypeStruct((n_mp, rounds, ROWS, width), bf16),
            jax.ShapeDtypeStruct((per_owner, rounds, ROWS, units), bf16),
        ),
        in_specs=[pl.BlockSpec(memory_space=pl.ANY)] * 2,
        out_specs=(
            pl.BlockSpec(memory_space=pl.ANY),
            pl.BlockSpec(memory_space=pltpu.VMEM),
        ),
        scratch_shapes=[
            pltpu.VMEM((rounds, n_mp, ROWS, width), bf16),
            pltpu.VMEM((units, width), bf16),
            pltpu.VMEM((rounds, n_mp, ROWS, units), bf16),
            pltpu.VMEM((n_dp - 1, rounds, per_owner, ROWS, units), bf16),
            dma, dma((chunks,)), dma((rounds,)),
            dma((rounds, 2, chips)), dma((rounds, 2, chips)),
            dma((rounds, 2, chips)), dma((rounds, 2, chips)),
            dma((n_dp - 1, rounds, chunks)), dma((n_dp - 1, rounds, chunks)),
        ],
        compiler_params=pltpu.CompilerParams(
            collective_id=0, has_side_effects=True, vmem_limit_bytes=56 * 1024 * 1024),
        cost_estimate=pl.CostEstimate(
            flops=2 * tokens * width * units, transcendentals=0,
            bytes_accessed=2 * units * width),
    )(grad_out.reshape(rounds, ROWS, width), down_weight)

    grad_weight = weight_gradient(hidden, panel.reshape(tokens, width))
    return gh.reshape(tokens // n_dp, units), grad_weight


def solution(mesh):
    return jax.shard_map(
        functools.partial(per_device, mesh.shape["dp"], mesh.shape["mp"]),
        mesh=mesh,
        in_specs=(P(None, "mp"), P("mp", "dp"), P("mp", "dp")),
        out_specs=(P("dp", "mp"), P("mp", "dp")),
        check_vma=False,
    )
```
